32 devices in a mesh: groups: 2 (over x), wide: 16 (over z, y, core).
Axes of the slice: x: 2, y: 2, z: 4, core: 2. Of those that a mesh axis runs over, the one named last changes fastest.
Arguments:
- features: bfloat16 [4096, 512], P(('groups', 'wide')), parts along dimension 0, may hold values from -3.5 to 3.5
- centres: bfloat16 [8192, 512], P(('groups', 'wide')), parts along dimension 0, may hold values from -3.5 to 3.5
- targets: bfloat16 [4096, 128], P(('groups', 'wide')), parts along dimension 0, may hold values from -8 to 8
- coefficients: float32 [8192, 128], P(('groups', 'wide')), parts along dimension 0, may hold values from -1.6 to 1.6
- momentum: float32 [8192, 128], P(('groups', 'wide')), parts along dimension 0, may hold values from -0.8 to 0.8
- block_inverse: float32 [32, 256, 256], P(('groups', 'wide')), parts along dimension 0, may hold values from -3 to 3
Outputs:
- residual: float32 [4096, 128], P(('groups', 'wide')), parts along dimension 0
- new_momentum: float32 [8192, 128], P(('groups', 'wide')), parts along dimension 0
- new_coefficients: float32 [8192, 128], P(('groups', 'wide')), parts along dimension 0
The draws below stay inside these ranges and needn't reach their ends.
There are 2 independent parts, one for each index of `groups`. The reference program is written for one: setup_inputs(seed, part) draws one part's arguments, and reference() takes and returns one part's arrays. A program takes and returns all parts, laid end to end along the dimension named above; each array names one. Nothing has to cross between parts.
All inputs are finite; a program needn't handle non-finite values.
Results may differ from the reference program's by a relative error of at most 0.0033.
Values may be sent and summed in bfloat16 or wider, within the bound.
No kernel may reach another device: no remote copies, remote signals or barrier semaphores. Data moves between devices by JAX's collectives and lax.ppermute only.
A program may use at most 128 MiB of HBM per device.

```python
import jax
import jax.numpy as jnp
from jax import lax

D = 512
OUTS = 128
BLOCK = 256
BATCH = 2048
CENTRES = 4096


def cluster_layout(key):
    clusters = max(CENTRES // 64, 4)
    supers = max(clusters // 32, 2)
    parent = jax.random.randint(jax.random.fold_in(key, 103), (clusters,), 0, supers)
    coarse = jax.random.normal(jax.random.fold_in(key, 101), (supers, D), jnp.float32) * 0.7071
    offset = jax.random.normal(jax.random.fold_in(key, 102), (clusters, D), jnp.float32) * 0.7071
    return (coarse[parent] + offset, clusters)


def draw_points(key, stream, row_count):
    cluster_mean, clusters = cluster_layout(key)
    member = jax.random.randint(jax.random.fold_in(key, stream), (row_count,), 0, clusters)
    jitter = jax.random.normal(jax.random.fold_in(key, stream + 1), (row_count, D), jnp.float32) * 0.4
    return jnp.clip(cluster_mean[member] + jitter, -3.5, 3.5).astype(jnp.bfloat16)


def draw_features(key, part):
    return draw_points(key, 1, BATCH)


def draw_centres(key, part):
    return draw_points(key, 3, CENTRES)


def with_spikes(result, key, source, target, shards_of, factor):
    owner, partner = [(jnp.arange(result.shape[axis_at]) // (result.shape[axis_at] // shards_of)).reshape([-1 if axis == axis_at else 1 for axis in range(result.ndim)]) for axis_at in (source, target)]
    chosen = jax.random.permutation(key, shards_of)[partner]
    strong = (owner == chosen) | (owner == (partner + shards_of // 2) % shards_of)
    return jnp.where(strong, factor * result, result)


def block_levels(key, extent, shards, low, high):
    def one(axis_at, parts):
        steps = jax.random.uniform(jax.random.fold_in(jax.random.fold_in(key, 6), axis_at), (parts,), jnp.float32, low / len(shards), high / len(shards))
        return jnp.repeat(jnp.exp(steps), extent[axis_at] // parts).reshape((-1,) + (1,) * (len(extent) - axis_at - 1))

    level = one(*shards[0])
    for cut in shards[1:]:
        level = level * one(*cut)
    return level


def normal_values(stream_key, dims, width, reach, cuts=(), dtype=jnp.bfloat16):
    array = jax.random.normal(stream_key, dims, jnp.float32) * width
    if len(cuts) > 0:
        array = block_levels(stream_key, dims, cuts, -0.22, 0.18) * array
    return jnp.clip(array, min=-reach, max=reach).astype(dtype)


def bell_draw_with(own_key, extent, width, reach, cuts, heavy, kind=jnp.bfloat16):
    drawn = width * jax.random.normal(own_key, extent, jnp.float32)
    if cuts:
        drawn = drawn * block_levels(own_key, extent, cuts, -0.22, 0.18)
    return jnp.clip(with_spikes(drawn, jax.random.fold_in(own_key, 3), *heavy), -reach, reach).astype(kind)


def setup_inputs(seed: int = 0, part: int = 0) -> dict:
    key_of = jax.random.split(jax.random.key(seed), 7)
    own_keys = jax.random.split(jax.random.fold_in(key_of[6], part), 7)
    return {
        "features": draw_features(jax.random.fold_in(jax.random.fold_in(key_of[6], part), 71), part),
        "centres": draw_centres(jax.random.fold_in(jax.random.fold_in(key_of[6], part), 71), part),
        "targets": bell_draw_with(own_keys[2], (BATCH, OUTS), 1.0, 8.0, ((0, 16),), (0, 1, 16, 2.0)),
        "coefficients": bell_draw_with(own_keys[3], (CENTRES, OUTS), 0.2, 1.6, ((0, 16),), (0, 1, 16, 2.0), jnp.float32),
        "momentum": normal_values(own_keys[4], (CENTRES, OUTS), 0.1, 0.8, ((0, 16),), jnp.float32),
        "block_inverse": normal_values(own_keys[5], (CENTRES // BLOCK, BLOCK, BLOCK), 4 ** -0.5, 3.0, ((0, 16),), jnp.float32),
    }


def kernel_tile(shard_rows, row_norms, centre_block):
    centre_norms = jnp.sum(centre_block.astype(jnp.float32) ** 2, axis=1)
    products = jnp.dot(shard_rows, centre_block.T, preferred_element_type=jnp.float32)
    return jnp.exp((2.0 * products - row_norms[:, None] - centre_norms[None, :]) * (2.0 / D)).astype(jnp.bfloat16)


def reference(features, centres, targets, coefficients, momentum, block_inverse):
    row_norms = jnp.sum(features.astype(jnp.float32) ** 2, axis=1)
    nblocks = CENTRES // BLOCK
    centre_blocks = centres.reshape(nblocks, BLOCK, D)
    coef_blocks = coefficients.astype(jnp.bfloat16).reshape(nblocks, BLOCK, OUTS)

    def accumulate(running, block_pair):
        centre_block, coef_block = block_pair
        kernel = kernel_tile(features, row_norms, centre_block)
        return running + jnp.dot(kernel, coef_block, preferred_element_type=jnp.float32), None

    prediction, _ = lax.scan(accumulate, jnp.zeros((BATCH, OUTS), jnp.float32), (centre_blocks, coef_blocks))
    residual = prediction - targets.astype(jnp.float32)
    residual_half = residual.astype(jnp.bfloat16)

    def gradient_block(centre_block):
        kernel = kernel_tile(features, row_norms, centre_block)
        return lax.dot_general(kernel, residual_half, (((0,), (0,)), ((), ())), preferred_element_type=jnp.float32)

    gradient = lax.map(gradient_block, centre_blocks)
    conditioned = jnp.einsum("bij,bjk->bik", block_inverse, gradient, precision=lax.Precision.HIGHEST)
    new_momentum = 0.9 * momentum + conditioned.reshape(CENTRES, OUTS) / BATCH
    new_coefficients = coefficients - 0.5 * new_momentum
    return residual, new_momentum, new_coefficients
```

```python
import functools

import jax
import jax.numpy as jnp
from jax import lax
from jax.experimental import pallas as pl
from jax.experimental.pallas import tpu as pltpu
from jax.sharding import PartitionSpec as P


F32, BF16 = jnp.float32, jnp.bfloat16
MIB = 1 << 20


def swap(x, mask, size):
    return lax.ppermute(x, "wide", [(i, i ^ mask) for i in range(size)])


def masks_of(bits):
    masks = [0]
    for bit in bits:
        masks += [m ^ bit for m in masks]
    return masks


def digits_of(bits):
    return [bits[i : i + 2] for i in range(0, len(bits), 2)]


def gather_pieces(x, digits, size):
    pieces = [x]
    for digit in digits:
        whole = pieces[0] if len(pieces) == 1 else jnp.concatenate(pieces)
        pieces = [whole] + [swap(whole, m, size) for m in masks_of(digit)[1:]]
    return pieces


def nbytes(*arrays):
    return sum(a.size * a.dtype.itemsize for a in arrays)


def whole_call(body, outs, args, scratch=(), flops=0):
    moved = nbytes(*args, *outs)
    return pl.pallas_call(
        body,
        out_shape=outs,
        in_specs=[pl.BlockSpec(memory_space=pltpu.VMEM)] * len(args),
        out_specs=[pl.BlockSpec(memory_space=pltpu.VMEM)] * len(outs),
        scratch_shapes=scratch,
        compiler_params=pltpu.CompilerParams(vmem_limit_bytes=moved + 12 * MIB),
        cost_estimate=pl.CostEstimate(flops=flops, bytes_accessed=moved, transcendentals=0),
    )(*args)


def predict_body(nrow, ncen, first, *refs):
    rows, refs = refs[:nrow], refs[nrow:]
    centres, refs = refs[:ncen], refs[ncen:]
    coefs, refs = refs[:ncen], refs[ncen:]
    given, refs = (refs[:1], refs[1:]) if first else (refs[:nrow], refs[nrow:])
    kernel_ref, sums = refs[0], refs[1:]
    width = rows[0].shape[1]
    order = centres[0].shape[0]
    chunk = 128
    norms = []
    ones = jnp.ones((8, width), BF16)
    for c in centres:
        square = c[...].astype(F32) ** 2
        high = square.astype(BF16)
        low = (square - high.astype(F32)).astype(BF16)
        dims = (((1,), (1,)), ((), ()))
        norm = lax.dot_general(ones, high, dims, preferred_element_type=F32)
        norm += lax.dot_general(ones, low, dims, preferred_element_type=F32)
        norms.append(norm[:1])
    base = 0
    for piece in range(nrow):
        count = rows[piece].shape[0] // chunk

        def step(i, base=base, piece=piece):
            at = pl.ds(i * chunk, chunk)
            x = rows[piece][at, :]
            row_norms = jnp.sum(x.astype(F32) ** 2, axis=1, keepdims=True)
            if not first:
                total = given[piece][at, :]
            elif piece == 0:
                total = jnp.where(i == 0, -1.0, 0.0) * given[0][...].astype(F32)
            else:
                total = jnp.zeros((chunk, sums[0].shape[1]), F32)
            for j in range(ncen):
                products = lax.dot_general(x, centres[j][...], (((1,), (1,)), ((), ())), preferred_element_type=F32)
                k = jnp.exp((2.0 * products - row_norms - norms[j]) * (2.0 / width)).astype(BF16)
                kernel_ref[pl.ds(base + i * chunk, chunk), j * order : (j + 1) * order] = k
                total += jnp.dot(k, coefs[j][...], preferred_element_type=F32)
            sums[piece][at, :] = total

        if count == 1:
            step(0)
        else:
            pl.loop(0, count)(step)
        base += count * chunk


def predict(rows, centres, coefs, given, first):
    total = sum(x.shape[0] for x in rows)
    depth = sum(c.shape[0] for c in centres)
    outs = [jax.ShapeDtypeStruct((total, depth), BF16)]
    outs += [jax.ShapeDtypeStruct((x.shape[0], coefs[0].shape[1]), F32) for x in rows]
    body = functools.partial(predict_body, len(rows), len(centres), first)
    flops = 2 * total * depth * (rows[0].shape[1] + coefs[0].shape[1])
    kernel, *sums = whole_call(body, outs, [*rows, *centres, *coefs, *given], flops=flops)
    return kernel, sums


def gradient_body(nker, npiece, *refs):
    kernels, refs = refs[:nker], refs[nker:]
    pieces, refs = refs[:npiece], refs[npiece:]
    keep, give, residual = refs
    base = 0
    for piece in pieces:
        residual[base : base + piece.shape[0], :] = piece[...]
        base += piece.shape[0]
    chunk = min(512, base)
    for n, kernel in enumerate(kernels):
        half = kernel.shape[1] // 2
        for side, out in ((0, keep), (1, give)):
            at = pl.ds(n * half, half)
            columns = slice(side * half, (side + 1) * half)

            def term(i, columns=columns, kernel=kernel):
                return lax.dot_general(
                    kernel[pl.ds(i * chunk, chunk), columns],
                    residual[pl.ds(i * chunk, chunk), :],
                    (((0,), (0,)), ((), ())),
                    preferred_element_type=F32,
                )

            out[at, :] = term(0)
            if base > chunk:

                @pl.loop(1, base // chunk)
                def _(i, out=out, at=at, term=term):
                    out[at, :] += term(i)


def gradients(kernels, pieces):
    total = kernels[0].shape[0]
    columns = pieces[0].shape[1]
    depth = sum(k.shape[1] for k in kernels)
    out = jax.ShapeDtypeStruct((depth // 2, columns), F32)
    body = functools.partial(gradient_body, len(kernels), len(pieces))
    return whole_call(
        body,
        [out, out],
        [*kernels, *pieces],
        scratch=[pltpu.VMEM((total, columns), BF16)],
        flops=2 * total * depth * columns,
    )


def update_body(batch, keep, arrived, inverse, momentum, coefficients, new_momentum, new_coefficients):
    gradient = keep[...] + arrived[...]
    nblocks, order = inverse.shape[0], inverse.shape[1]
    for b in range(nblocks):
        at = slice(b * order, (b + 1) * order)
        conditioned = jnp.dot(
            inverse[b], gradient[at], precision=lax.Precision.HIGHEST, preferred_element_type=F32
        )
        moved = 0.9 * momentum[at, :] + conditioned / batch
        new_momentum[at, :] = moved
        new_coefficients[at, :] = coefficients[at, :] - 0.5 * moved


def shards(size, features, centres, targets, coefficients, momentum, block_inverse):
    batch = features.shape[0] * size
    count = centres.shape[0]
    core, far = 1, size // 2
    digits = digits_of([1 << b for b in range(1, size.bit_length() - 2)])
    send = functools.partial(swap, size=size)

    coef_half = coefficients.astype(BF16)
    far_centres, far_coef = send(centres, far), send(coef_half, far)
    rows = gather_pieces(features, digits, size)
    near = [centres, send(centres, core)]
    near_coef = [coef_half, send(coef_half, core)]
    kernel_near, sums = predict(rows, near, near_coef, [targets], True)
    far_centres, far_coef, sums = lax.optimization_barrier((far_centres, far_coef, sums))
    distant = [far_centres, send(far_centres, core)]
    distant_coef = [far_coef, send(far_coef, core)]
    kernel_far, sums = predict(rows, distant, distant_coef, sums, False)

    for digit in reversed(digits):
        masks = masks_of(digit)
        if len(sums) == 1:
            sums = jnp.split(sums[0], len(masks))
        total = sums[0]
        for m, part in zip(masks[1:], sums[1:]):
            total = total + send(part, m)
        sums = [total]
    residual = sums[0]
    residuals = gather_pieces(residual.astype(BF16), digits, size)

    keep, give = gradients([kernel_near, kernel_far], residuals)
    both = keep + send(give, core)
    arrived = send(both[count:], far)
    out = jax.ShapeDtypeStruct(momentum.shape, F32)
    new_momentum, new_coefficients = whole_call(
        functools.partial(update_body, batch),
        [out, out],
        [both[:count], arrived, block_inverse, momentum, coefficients],
    )
    return residual, new_momentum, new_coefficients


def solution(mesh):
    one = P(("groups", "wide"), None)
    in_specs = (one, one, one, one, one, P(("groups", "wide"), None, None))
    return jax.shard_map(
        functools.partial(shards, mesh.shape["wide"]),
        mesh=mesh,
        in_specs=in_specs,
        out_specs=(one, one, one),
        check_vma=False,
    )
```

```python
import functools

import jax
import jax.numpy as jnp
from jax import lax
from jax.experimental import pallas as pl
from jax.experimental.pallas import tpu as pltpu
from jax.sharding import PartitionSpec as P


F32, BF16 = jnp.float32, jnp.bfloat16
MIB = 1 << 20


def swap(x, mask, size):
    return lax.ppermute(x, "wide", [(i, i ^ mask) for i in range(size)])


def masks_of(bits):
    masks = [0]
    for bit in bits:
        masks += [m ^ bit for m in masks]
    return masks


def digits_of(bits):
    return [bits[i : i + 2] for i in range(0, len(bits), 2)]


def gather_pieces(x, digits, size):
    pieces = [x]
    for digit in digits:
        whole = pieces[0] if len(pieces) == 1 else jnp.concatenate(pieces)
        pieces = [whole] + [swap(whole, m, size) for m in masks_of(digit)[1:]]
    return pieces


def nbytes(*arrays):
    return sum(a.size * a.dtype.itemsize for a in arrays)


def whole_call(body, outs, args, scratch=(), flops=0):
    moved = nbytes(*args, *outs)
    return pl.pallas_call(
        body,
        out_shape=outs,
        in_specs=[pl.BlockSpec(memory_space=pltpu.VMEM)] * len(args),
        out_specs=[pl.BlockSpec(memory_space=pltpu.VMEM)] * len(outs),
        scratch_shapes=scratch,
        compiler_params=pltpu.CompilerParams(vmem_limit_bytes=moved + 12 * MIB),
        cost_estimate=pl.CostEstimate(flops=flops, bytes_accessed=moved, transcendentals=0),
    )(*args)


def prepare_body(features, centres, coefficients, rows, blocks, weights):
    rows[...] = features[...]
    blocks[...] = centres[...]
    weights[...] = coefficients[...].astype(BF16)


def prepare(features, centres, coefficients):
    outs = [jax.ShapeDtypeStruct(x.shape, BF16) for x in (features, centres, coefficients)]
    return whole_call(prepare_body, outs, [features, centres, coefficients])


def predict_body(nrow, ncen, first, *refs):
    rows, refs = refs[:nrow], refs[nrow:]
    blocks, refs = refs[:ncen], refs[ncen:]
    weights, refs = refs[:ncen], refs[ncen:]
    given, refs = ((), refs) if first else (refs[:nrow], refs[nrow:])
    kernel_ref, sums = refs[0], refs[1:]
    width = rows[0].shape[1]
    centres = jnp.concatenate([block[...] for block in blocks])
    coefs = jnp.concatenate([weight[...].astype(BF16) for weight in weights])
    dims = (((1,), (1,)), ((), ()))
    square = centres.astype(F32) ** 2
    high = square.astype(BF16)
    low = (square - high.astype(F32)).astype(BF16)
    ones = jnp.ones((8, width), BF16)
    norms = lax.dot_general(ones, high, dims, preferred_element_type=F32)
    norms = (norms + lax.dot_general(ones, low, dims, preferred_element_type=F32))[:1]

    def tile(x, at):
        row_norms = jnp.sum(x.astype(F32) ** 2, axis=1, keepdims=True)
        products = lax.dot_general(x, centres, dims, preferred_element_type=F32)
        k = jnp.exp((2.0 * products - row_norms - norms) * (2.0 / width)).astype(BF16)
        kernel_ref[at, :] = k
        return jnp.dot(k, coefs, preferred_element_type=F32)

    sizes = [x.shape[0] for x in rows]
    if sum(sizes) <= 512:
        part = tile(jnp.concatenate([x[...] for x in rows]), slice(None))
        starts = [sum(sizes[:n]) for n in range(nrow)]
        for n, start in enumerate(starts):
            sums[n][...] = part[start : start + sizes[n]]
    else:
        base = 0
        for x, out in zip(rows, sums):
            chunk = min(512, x.shape[0])

            @pl.loop(0, x.shape[0] // chunk)
            def _(i, x=x, out=out, base=base, chunk=chunk):
                at = pl.ds(i * chunk, chunk)
                out[at, :] = tile(x[at, :], pl.ds(base + i * chunk, chunk))

            base += x.shape[0]
    for out, before in zip(sums, given):
        out[...] += before[...]


def predict(rows, blocks, given=(), flops=None):
    blocks, weights = zip(*blocks)
    total = sum(x.shape[0] for x in rows)
    depth = sum(b.shape[0] for b in blocks)
    width = rows[0].shape[1]
    outs = weights[0].shape[1]
    shapes = [jax.ShapeDtypeStruct((total, depth), BF16)]
    shapes += [jax.ShapeDtypeStruct((x.shape[0], outs), F32) for x in rows]
    body = functools.partial(predict_body, len(rows), len(blocks), not given)
    flops = flops or 2 * total * depth * (width + outs)
    kernel, *sums = whole_call(body, shapes, [*rows, *blocks, *weights, *given], flops=flops)
    return kernel, sums


def gradient_body(layout, npiece, *refs):
    kernels, refs = refs[: len(layout)], refs[len(layout) :]
    pieces, refs = refs[:npiece], refs[npiece:]
    *outs, residual = refs
    base = 0
    for piece in pieces:
        residual[base : base + piece.shape[0], :] = piece[...]
        base += piece.shape[0]
    started = set()
    for kernel, (first_row, columns) in zip(kernels, layout):
        rows, depth = kernel.shape
        order = depth // len(columns)
        chunk = min(512, rows)
        for n, (out, place) in enumerate(columns):
            at = slice(place * order, (place + 1) * order)

            def term(i, kernel=kernel, n=n, first_row=first_row, chunk=chunk, order=order):
                return lax.dot_general(
                    kernel[pl.ds(i * chunk, chunk), n * order : (n + 1) * order],
                    residual[pl.ds(first_row + i * chunk, chunk), :],
                    (((0,), (0,)), ((), ())),
                    preferred_element_type=F32,
                )

            if (out, place) in started:
                outs[out][at, :] += term(0)
            else:
                outs[out][at, :] = term(0)
                started.add((out, place))
            if rows > chunk:

                @pl.loop(1, rows // chunk)
                def _(i, out=out, at=at, term=term):
                    outs[out][at, :] += term(i)


def gradients(kernels, layout, pieces, count):
    total = sum(p.shape[0] for p in pieces)
    columns = pieces[0].shape[1]
    out = jax.ShapeDtypeStruct((2 * count, columns), F32)
    body = functools.partial(gradient_body, layout, len(pieces))
    return whole_call(
        body,
        [out, out],
        [*kernels, *pieces],
        scratch=[pltpu.VMEM((total, columns), BF16)],
        flops=8 * total * count * columns,
    )


def update_body(batch, keep, arrived, inverse, momentum, coefficients, new_momentum, new_coefficients):
    gradient = keep[...] + arrived[...]
    nblocks, order = inverse.shape[0], inverse.shape[1]
    for b in range(nblocks):
        at = slice(b * order, (b + 1) * order)
        conditioned = jnp.dot(
            inverse[b], gradient[at], precision=lax.Precision.HIGHEST, preferred_element_type=F32
        )
        moved = 0.9 * momentum[at, :] + conditioned / batch
        new_momentum[at, :] = moved
        new_coefficients[at, :] = coefficients[at, :] - 0.5 * moved


def shards(size, features, centres, targets, coefficients, momentum, block_inverse):
    batch = features.shape[0] * size
    count = centres.shape[0]
    core, far = 1, 2
    digits = digits_of([1 << b for b in range(1, size.bit_length() - 1) if 1 << b != far])
    send = functools.partial(swap, size=size)

    own_rows, *own = prepare(features, centres, coefficients)
    rows = gather_pieces(features, digits, size)
    if len(digits) == 1:
        rows[0] = own_rows
    far_block = [send(centres, far), send(coefficients, far)]
    near = [send(centres, core), send(coefficients, core)]
    kernel_a, sums_a = predict(rows, [own], flops=4 * 10**9)
    kernel_b, sums_b = predict(rows, [near], sums_a)
    far_block, rows[-1] = lax.optimization_barrier((far_block, rows[-1]))
    distant = [far_block, [send(x, core) for x in far_block]]
    kernel_c, sums = predict(rows, distant, sums_b)
    kernels = [kernel_a, kernel_b, kernel_c]
    layout = ((0, ((0, 0),)), (0, ((1, 0),)), (0, ((0, 1), (1, 1))))

    for digit in reversed(digits):
        masks = masks_of(digit)
        if len(sums) == 1:
            sums = jnp.split(sums[0], len(masks))
        total = sums[0]
        for m, part in zip(masks[1:], sums[1:]):
            total = total + send(part, m)
        sums = [total]
    residual = sums[0] - targets.astype(F32)
    residuals = gather_pieces(residual.astype(BF16), digits, size)

    keep, give = gradients(kernels, layout, residuals, count)
    both = keep + send(give, core)
    arrived = send(both[count:], far)
    out = jax.ShapeDtypeStruct(momentum.shape, F32)
    new_momentum, new_coefficients = whole_call(
        functools.partial(update_body, batch),
        [out, out],
        [both[:count], arrived, block_inverse, momentum, coefficients],
    )
    return residual, new_momentum, new_coefficients


def solution(mesh):
    one = P(("groups", "wide"), None)
    in_specs = (one, one, one, one, one, P(("groups", "wide"), None, None))
    return jax.shard_map(
        functools.partial(shards, mesh.shape["wide"]),
        mesh=mesh,
        in_specs=in_specs,
        out_specs=(one, one, one),
        check_vma=False,
    )
```

```python
import functools

import jax
import jax.numpy as jnp
from jax import lax
from jax.experimental import pallas as pl
from jax.experimental.pallas import tpu as pltpu
from jax.sharding import PartitionSpec as P


F32, BF16 = jnp.float32, jnp.bfloat16
MIB = 1 << 20
SUM_ORDER = (3, 1, 2, 0)
GATHER_ORDER = (0, 1, 2, 3)
ROW_ORDER = (0, 1, 2, 3)


def swap(x, mask, size):
    return lax.ppermute(x, "wide", [(i, i ^ mask) for i in range(size)])


def masks_of(bits):
    masks = [0]
    for bit in bits:
        masks += [m ^ bit for m in masks]
    return masks


def digits_of(bits):
    return [bits[i : i + 2] for i in range(0, len(bits), 2)]


def gather_pieces(x, digits, size):
    pieces = [x]
    for digit in digits:
        whole = pieces[0] if len(pieces) == 1 else jnp.concatenate(pieces)
        pieces = [whole] + [swap(whole, m, size) for m in masks_of(digit)[1:]]
    return pieces


def relay_pieces(x, digits, size):
    pieces = [x]
    for digit in digits:
        pieces = [pieces[0] if len(pieces) == 1 else jnp.concatenate(pieces)]
        if len(digit) == 2:
            far = swap(pieces[0], digit[1], size)
            pieces += [swap(pieces[0], digit[0], size), far, swap(far, digit[0], size)]
        else:
            pieces += [swap(pieces[0], digit[0], size)]
    return pieces


def in_order(items, order):
    return [items[order.index(n)] for n in range(len(items))] if len(order) == len(items) else list(items)


def put(items, order):
    return [items[n] for n in order] if len(order) == len(items) else list(items)


def nbytes(*arrays):
    return sum(a.size * a.dtype.itemsize for a in arrays)


def whole_call(body, outs, args, scratch=(), flops=0):
    moved = nbytes(*args, *outs)
    return pl.pallas_call(
        body,
        out_shape=outs,
        in_specs=[pl.BlockSpec(memory_space=pltpu.VMEM)] * len(args),
        out_specs=[pl.BlockSpec(memory_space=pltpu.VMEM)] * len(outs),
        scratch_shapes=scratch,
        compiler_params=pltpu.CompilerParams(vmem_limit_bytes=moved + 12 * MIB),
        cost_estimate=pl.CostEstimate(flops=flops, bytes_accessed=moved, transcendentals=0),
    )(*args)


def prepare_body(features, centres, coefficients, rows, blocks, weights):
    rows[...] = features[...]
    blocks[...] = centres[...]
    weights[...] = coefficients[...].astype(BF16)


def prepare(features, centres, coefficients):
    outs = [jax.ShapeDtypeStruct(x.shape, BF16) for x in (features, centres, coefficients)]
    return whole_call(prepare_body, outs, [features, centres, coefficients])


def predict_body(nrow, ncen, nweight, first, *refs):
    rows, refs = in_order(refs[:nrow], ROW_ORDER), refs[nrow:]
    blocks, refs = refs[:ncen], refs[ncen:]
    weights, refs = refs[:nweight], refs[nweight:]
    given, refs = ((), refs) if first else (refs[:nrow], refs[nrow:])
    kernel_ref, sums = refs[0], refs[1:]
    width = rows[0].shape[1]
    centres = jnp.concatenate([block[...] for block in blocks])
    coefs = jnp.concatenate([weight[...].astype(BF16) for weight in weights])
    dims = (((1,), (1,)), ((), ()))
    square = centres.astype(F32) ** 2
    high = square.astype(BF16)
    low = (square - high.astype(F32)).astype(BF16)
    ones = jnp.ones((8, width), BF16)
    norms = lax.dot_general(ones, high, dims, preferred_element_type=F32)
    norms = (norms + lax.dot_general(ones, low, dims, preferred_element_type=F32))[:1]

    def tile(x, at):
        row_norms = jnp.sum(x.astype(F32) ** 2, axis=1, keepdims=True)
        products = lax.dot_general(x, centres, dims, preferred_element_type=F32)
        k = jnp.exp((2.0 * products - row_norms - norms) * (2.0 / width)).astype(BF16)
        kernel_ref[at, :] = k
        return jnp.dot(k, coefs, preferred_element_type=F32)

    sizes = [x.shape[0] for x in rows]
    if sum(sizes) <= 512:
        part = tile(jnp.concatenate([x[...] for x in rows]), slice(None))
        starts = [sum(sizes[:n]) for n in range(nrow)]
        for n, start in enumerate(starts):
            sums[n][...] = part[start : start + sizes[n]]
    else:
        base = 0
        for x, out in zip(rows, sums):
            chunk = min(512, x.shape[0])

            @pl.loop(0, x.shape[0] // chunk)
            def _(i, x=x, out=out, base=base, chunk=chunk):
                at = pl.ds(i * chunk, chunk)
                out[at, :] = tile(x[at, :], pl.ds(base + i * chunk, chunk))

            base += x.shape[0]
    for out, before in zip(sums, given):
        out[...] += before[...]


def predict(rows, blocks, given=(), flops=None):
    blocks, weights = blocks
    total = sum(x.shape[0] for x in rows)
    depth = sum(b.shape[0] for b in blocks)
    width = rows[0].shape[1]
    outs = weights[0].shape[1]
    shapes = [jax.ShapeDtypeStruct((total, depth), BF16)]
    shapes += [jax.ShapeDtypeStruct((x.shape[0], outs), F32) for x in rows]
    body = functools.partial(predict_body, len(rows), len(blocks), len(weights), not given)
    flops = flops or 2 * total * depth * (width + outs)
    kernel, *sums = whole_call(body, shapes, [*put(rows, ROW_ORDER), *blocks, *weights, *given], flops=flops)
    return kernel, sums


def gradient_body(layout, npiece, nout, *refs):
    kernels, refs = refs[: len(layout)], refs[len(layout) :]
    pieces, refs = in_order(refs[:npiece], GATHER_ORDER), refs[npiece:]
    *outs, residual = refs
    base = 0
    for piece in pieces:
        residual[base : base + piece.shape[0], :] = piece[...]
        base += piece.shape[0]
    started = set()
    for kernel, (first_row, first_block, blocks) in zip(kernels, layout):
        rows, order = kernel.shape[0], outs[0].shape[0]
        chunk = min(512, rows)
        for n, out in enumerate(blocks, first_block):

            def term(i, kernel=kernel, n=n, first_row=first_row, chunk=chunk):
                return lax.dot_general(
                    kernel[pl.ds(i * chunk, chunk), n * order : (n + 1) * order],
                    residual[pl.ds(first_row + i * chunk, chunk), :],
                    (((0,), (0,)), ((), ())),
                    preferred_element_type=F32,
                )

            if out in started:
                outs[out][...] += term(0)
            else:
                outs[out][...] = term(0)
                started.add(out)
            if rows > chunk:

                @pl.loop(1, rows // chunk)
                def _(i, out=out, term=term):
                    outs[out][...] += term(i)


def gradients(kernels, layout, pieces, count, nout=2):
    total = sum(p.shape[0] for p in pieces)
    columns = pieces[0].shape[1]
    out = jax.ShapeDtypeStruct((count, columns), F32)
    body = functools.partial(gradient_body, layout, len(pieces), nout)
    return whole_call(
        body,
        [out] * nout,
        [*kernels, *put(pieces, GATHER_ORDER)],
        scratch=[pltpu.VMEM((total, columns), BF16)],
        flops=4 * total * count * columns,
    )


def residual_body(npart, *refs):
    *parts, targets, residual, half = refs
    parts = in_order(parts, SUM_ORDER)
    total = parts[0][...]
    for part in parts[1:]:
        total += part[...]
    total -= targets[...].astype(F32)
    residual[...] = total
    half[...] = total.astype(BF16)


def update_body(batch, npart, *refs):
    parts, refs = refs[:npart], refs[npart:]
    inverse, momentum, coefficients, residual, new_momentum, new_coefficients, out = refs
    out[...] = residual[...]
    gradient = parts[0][...]
    for part in parts[1:]:
        gradient += part[...]
    nblocks, order = inverse.shape[0], inverse.shape[1]
    for b in range(nblocks):
        at = slice(b * order, (b + 1) * order)
        conditioned = jnp.dot(
            inverse[b], gradient[at], precision=lax.Precision.HIGHEST, preferred_element_type=F32
        )
        moved = 0.9 * momentum[at, :] + conditioned / batch
        new_momentum[at, :] = moved
        new_coefficients[at, :] = coefficients[at, :] - 0.5 * moved


def shards(size, features, centres, targets, coefficients, momentum, block_inverse):
    batch = features.shape[0] * size
    count = centres.shape[0]
    core, far = 1, 2
    digits = digits_of([1 << b for b in range(1, size.bit_length() - 1) if 1 << b != far])
    send = functools.partial(swap, size=size)

    own_rows, *own = prepare(features, centres, coefficients)
    rows = relay_pieces(features, digits, size)
    if len(digits) == 1:
        rows[0] = own_rows
    coefficients_ = coefficients
    far_parts = [send(part, far) for part in jnp.split(centres, 2)]
    far_coef = send(coefficients_, far)
    near = [send(centres, core)], [send(coefficients_, core)]
    own = own[:1], own[1:]
    kernel_a, sums_a = predict(rows, own, flops=4 * 10**9)
    kernel_b, sums_b = predict(rows, near, sums_a, flops=None)
    far_parts, far_coef, rows[-2] = lax.optimization_barrier((far_parts, far_coef, rows[-2]))
    distant = far_parts + [send(x, core) for x in far_parts], [far_coef, send(far_coef, core)]
    kernel_c, sums = predict(rows, distant, sums_b)
    far_kernels, far_layout = [kernel_c], ((0, 0, (0, 1)),)
    near_kernels, near_layout = [kernel_a, kernel_b], ((0, 0, (0,)), (0, 0, (1,)))

    for digit in reversed(digits):
        masks = masks_of(digit)
        if len(sums) == 1:
            sums = jnp.split(sums[0], len(masks))
        terms = [sums[0]] + [send(part, m) for m, part in zip(masks[1:], sums[1:])]
        sums = [functools.reduce(jnp.add, terms)] if digit is not digits[0] else terms
    held = jax.ShapeDtypeStruct(targets.shape, F32)
    residual, half = whole_call(
        functools.partial(residual_body, len(sums)),
        [held, jax.ShapeDtypeStruct(targets.shape, BF16)],
        [*put(sums, SUM_ORDER), targets],
    )
    residuals = gather_pieces(half, digits, size)

    layout = far_layout + tuple((r, c, tuple(o + 2 for o in out)) for r, c, out in near_layout)
    far_keep, far_give, keep, give = gradients(far_kernels + near_kernels, layout, residuals, count, 4)
    far_got, got = send(far_give, core), send(give, core)
    parts = [keep, got, send(far_keep + far_got, far)]
    out = jax.ShapeDtypeStruct(momentum.shape, F32)
    new_momentum, new_coefficients, residual = whole_call(
        functools.partial(update_body, batch, len(parts)),
        [out, out, held],
        [*parts, block_inverse, momentum, coefficients, residual],
    )
    return residual, new_momentum, new_coefficients


def solution(mesh):
    one = P(("groups", "wide"), None)
    in_specs = (one, one, one, one, one, P(("groups", "wide"), None, None))
    return jax.shard_map(
        functools.partial(shards, mesh.shape["wide"]),
        mesh=mesh,
        in_specs=in_specs,
        out_specs=(one, one, one),
        check_vma=False,
    )
```

```python
import functools
import math

import jax
import jax.numpy as jnp
from jax import lax
from jax.experimental import pallas as pl
from jax.experimental.pallas import tpu as pltpu
from jax.sharding import PartitionSpec as P


F32, BF16 = jnp.float32, jnp.bfloat16
MIB = 1 << 20


def swap(x, mask, size):
    return lax.ppermute(x, "wide", [(i, i ^ mask) for i in range(size)])


def masks_of(bits):
    masks = [0]
    for bit in bits:
        masks += [m ^ bit for m in masks]
    return masks


def digits_of(bits):
    return [bits[i : i + 2] for i in range(0, len(bits), 2)]


def gather_pieces(x, digits, size):
    pieces = [x]
    for digit in digits:
        whole = pieces[0] if len(pieces) == 1 else jnp.concatenate(pieces)
        pieces = [whole] + [swap(whole, m, size) for m in masks_of(digit)[1:]]
    return pieces


def relay_pieces(x, digits, size):
    pieces = [x]
    for digit in digits:
        pieces = [pieces[0] if len(pieces) == 1 else jnp.concatenate(pieces)]
        if len(digit) == 2:
            far = swap(pieces[0], digit[1], size)
            pieces += [swap(pieces[0], digit[0], size), far, swap(far, digit[0], size)]
        else:
            pieces += [swap(pieces[0], digit[0], size)]
    return pieces


def nbytes(*arrays):
    return sum(a.size * a.dtype.itemsize for a in arrays)


def whole_call(body, outs, args, scratch=(), flops=0):
    moved = nbytes(*args, *outs)
    return pl.pallas_call(
        body,
        out_shape=outs,
        in_specs=[pl.BlockSpec(memory_space=pltpu.VMEM)] * len(args),
        out_specs=[pl.BlockSpec(memory_space=pltpu.VMEM)] * len(outs),
        scratch_shapes=scratch,
        compiler_params=pltpu.CompilerParams(vmem_limit_bytes=moved + 12 * MIB),
        cost_estimate=pl.CostEstimate(flops=flops, bytes_accessed=moved, transcendentals=0),
    )(*args)


def prepare_body(features, centres, coefficients, rows, blocks, weights):
    rows[...] = features[...]
    blocks[...] = centres[...]
    weights[...] = coefficients[...].astype(BF16)


def prepare(features, centres, coefficients):
    outs = [jax.ShapeDtypeStruct(x.shape, BF16) for x in (features, centres, coefficients)]
    return whole_call(prepare_body, outs, [features, centres, coefficients])


def predict_body(nrow, ncen, nweight, first, *refs):
    rows, refs = refs[:nrow], refs[nrow:]
    blocks, refs = refs[:ncen], refs[ncen:]
    weights, refs = refs[:nweight], refs[nweight:]
    given, refs = ((), refs) if first else (refs[:nrow], refs[nrow:])
    kernel_ref, sums = refs[0], refs[1:]
    width = rows[0].shape[1]
    centres = jnp.concatenate([block[...] for block in blocks])
    coefs = jnp.concatenate([weight[...].astype(BF16) for weight in weights])
    dims = (((1,), (1,)), ((), ()))
    norms = jnp.sum(centres.astype(F32) ** 2, axis=1, keepdims=True)
    norms = jnp.transpose(jnp.broadcast_to(norms, (centres.shape[0], 128)))[:1]

    def tile(x, at):
        row_norms = jnp.sum(x.astype(F32) ** 2, axis=1, keepdims=True)
        products = lax.dot_general(x, centres, dims, preferred_element_type=F32)
        k = jnp.exp((2.0 * products - row_norms - norms) * (2.0 / width)).astype(BF16)
        kernel_ref[at, :] = k
        return jnp.dot(k, coefs, preferred_element_type=F32)

    sizes = [x.shape[0] for x in rows]
    if sum(sizes) <= 512:
        part = tile(jnp.concatenate([x[...] for x in rows]), slice(None))
        starts = [sum(sizes[:n]) for n in range(nrow)]
        for n, start in enumerate(starts):
            sums[n][...] = part[start : start + sizes[n]]
    else:
        base = 0
        for x, out in zip(rows, sums):
            chunk = min(512, x.shape[0])

            @pl.loop(0, x.shape[0] // chunk)
            def _(i, x=x, out=out, base=base, chunk=chunk):
                at = pl.ds(i * chunk, chunk)
                out[at, :] = tile(x[at, :], pl.ds(base + i * chunk, chunk))

            base += x.shape[0]
    for out, before in zip(sums, given):
        out[...] += before[...]


def predict(rows, blocks, given=(), flops=None):
    blocks, weights = blocks
    total = sum(x.shape[0] for x in rows)
    depth = sum(b.shape[0] for b in blocks)
    width = rows[0].shape[1]
    outs = weights[0].shape[1]
    shapes = [jax.ShapeDtypeStruct((total, depth), BF16)]
    shapes += [jax.ShapeDtypeStruct((x.shape[0], outs), F32) for x in rows]
    body = functools.partial(predict_body, len(rows), len(blocks), len(weights), not given)
    flops = flops or 2 * total * depth * (width + outs)
    kernel, *sums = whole_call(body, shapes, [*rows, *blocks, *weights, *given], flops=flops)
    return kernel, sums


def gradient_body(layout, npiece, nout, *refs):
    kernels, refs = refs[: len(layout)], refs[len(layout) :]
    pieces, refs = refs[:npiece], refs[npiece:]
    *outs, residual = refs
    base = 0
    for piece in pieces:
        residual[base : base + piece.shape[0], :] = piece[...]
        base += piece.shape[0]
    started = set()
    for kernel, (first_row, first_block, blocks) in zip(kernels, layout):
        rows, order = kernel.shape[0], outs[0].shape[0]
        chunk = min(512, rows)
        for n, out in enumerate(blocks, first_block):

            def term(i, kernel=kernel, n=n, first_row=first_row, chunk=chunk):
                return lax.dot_general(
                    kernel[pl.ds(i * chunk, chunk), n * order : (n + 1) * order],
                    residual[pl.ds(first_row + i * chunk, chunk), :],
                    (((0,), (0,)), ((), ())),
                    preferred_element_type=F32,
                )

            if out in started:
                outs[out][...] += term(0)
            else:
                outs[out][...] = term(0)
                started.add(out)
            if rows > chunk:

                @pl.loop(1, rows // chunk)
                def _(i, out=out, term=term):
                    outs[out][...] += term(i)


def gradients(kernels, layout, pieces, count, nout=2):
    total = sum(p.shape[0] for p in pieces)
    columns = pieces[0].shape[1]
    out = jax.ShapeDtypeStruct((count, columns), F32)
    body = functools.partial(gradient_body, layout, len(pieces), nout)
    return whole_call(
        body,
        [out] * nout,
        [*kernels, *pieces],
        scratch=[pltpu.VMEM((total, columns), BF16)],
        flops=4 * total * count * columns,
    )


def update_body(batch, npart, *refs):
    parts, refs = refs[:npart], refs[npart:]
    inverse, momentum, coefficients, residual, new_momentum, new_coefficients, out = refs
    out[...] = residual[...]
    gradient = parts[0][...]
    for part in parts[1:]:
        gradient += part[...]
    nblocks, order = inverse.shape[0], inverse.shape[1]
    for b in range(nblocks):
        at = slice(b * order, (b + 1) * order)
        conditioned = jnp.dot(
            inverse[b], gradient[at], precision=lax.Precision.HIGHEST, preferred_element_type=F32
        )
        moved = 0.9 * momentum[at, :] + conditioned / batch
        new_momentum[at, :] = moved
        new_coefficients[at, :] = coefficients[at, :] - 0.5 * moved


def shards(size, features, centres, targets, coefficients, momentum, block_inverse):
    batch = features.shape[0] * size
    count = centres.shape[0]
    core, far = 1, 2
    digits = digits_of([1 << b for b in range(1, size.bit_length() - 1) if 1 << b != far])
    send = functools.partial(swap, size=size)

    own_rows, *own = prepare(features, centres, coefficients)
    rows = relay_pieces(features, digits, size)
    if len(digits) == 1:
        rows[0] = own_rows
    far_parts = [send(part, far) for part in jnp.split(centres, 2)]
    far_coef = send(coefficients, far)
    near = [send(centres, core)], [send(coefficients, core)]
    own = own[:1], own[1:]
    kernel_a, sums_a = predict(rows, own, flops=4 * 10**9)
    kernel_b, sums_b = predict(rows, near, sums_a)
    far_parts, far_coef, rows[-2] = lax.optimization_barrier((far_parts, far_coef, rows[-2]))
    distant = far_parts + [send(x, core) for x in far_parts], [far_coef, send(far_coef, core)]
    kernel_c, sums = predict(rows, distant, sums_b)
    far_kernels, far_layout = [kernel_c], ((0, 0, (0, 1)),)
    near_kernels, near_layout = [kernel_a, kernel_b], ((0, 0, (0,)), (0, 0, (1,)))

    scale = 2.0 ** math.floor(math.log2(65504 / (5.05 * 4 * count)))
    for digit in reversed(digits):
        masks = masks_of(digit)
        if len(sums) == 1:
            sums = jnp.split(sums[0], len(masks))
        kind, factor = (jnp.float16, scale) if digit is digits[-1] else (F32, 1.0)
        sent = [(factor * part).astype(kind) for part in sums[1:]]
        got = [send(part, m).astype(F32) for m, part in zip(masks[1:], sent)]
        sums = [sums[0] + functools.reduce(jnp.add, got) / factor]
    residual = sums[0] - targets.astype(F32)
    half = residual.astype(BF16)
    held = jax.ShapeDtypeStruct(targets.shape, F32)
    residuals = gather_pieces(half, digits, size)

    layout = far_layout + tuple((r, c, tuple(o + 2 for o in out)) for r, c, out in near_layout)
    far_keep, far_give, keep, give = gradients(far_kernels + near_kernels, layout, residuals, count, 4)
    far_got, got = send(far_give, core), send(give, core)
    parts = [keep, got, send(far_keep + far_got, far)]
    out = jax.ShapeDtypeStruct(momentum.shape, F32)
    new_momentum, new_coefficients, residual = whole_call(
        functools.partial(update_body, batch, len(parts)),
        [out, out, held],
        [*parts, block_inverse, momentum, coefficients, residual],
    )
    return residual, new_momentum, new_coefficients


def solution(mesh):
    one = P(("groups", "wide"), None)
    in_specs = (one, one, one, one, one, P(("groups", "wide"), None, None))
    return jax.shard_map(
        functools.partial(shards, mesh.shape["wide"]),
        mesh=mesh,
        in_specs=in_specs,
        out_specs=(one, one, one),
        check_vma=False,
    )
```

```python
import functools
import math

import jax
import jax.numpy as jnp
from jax import lax
from jax.experimental import pallas as pl
from jax.experimental.pallas import tpu as pltpu
from jax.sharding import PartitionSpec as P


F32, BF16 = jnp.float32, jnp.bfloat16
MIB = 1 << 20


def swap(x, mask, size):
    return lax.ppermute(x, "wide", [(i, i ^ mask) for i in range(size)])


def masks_of(bits):
    masks = [0]
    for bit in bits:
        masks += [m ^ bit for m in masks]
    return masks


def digits_of(bits):
    return [bits[i : i + 2] for i in range(0, len(bits), 2)]


def gather_pieces(x, digits, size):
    pieces = [x]
    for digit in digits:
        whole = pieces[0] if len(pieces) == 1 else jnp.concatenate(pieces)
        pieces = [whole] + [swap(whole, m, size) for m in masks_of(digit)[1:]]
    return pieces


def relay_pieces(x, digits, size):
    pieces = [x]
    for digit in digits:
        pieces = [pieces[0] if len(pieces) == 1 else jnp.concatenate(pieces)]
        if len(digit) == 2:
            far = swap(pieces[0], digit[1], size)
            pieces += [swap(pieces[0], digit[0], size), far, swap(far, digit[0], size)]
        else:
            pieces += [swap(pieces[0], digit[0], size)]
    return pieces


def nbytes(*arrays):
    return sum(a.size * a.dtype.itemsize for a in arrays)


def whole_call(body, outs, args, scratch=(), flops=0):
    moved = nbytes(*args, *outs)
    return pl.pallas_call(
        body,
        out_shape=outs,
        in_specs=[pl.BlockSpec(memory_space=pltpu.VMEM)] * len(args),
        out_specs=[pl.BlockSpec(memory_space=pltpu.VMEM)] * len(outs),
        scratch_shapes=scratch,
        compiler_params=pltpu.CompilerParams(vmem_limit_bytes=moved + 12 * MIB),
        cost_estimate=pl.CostEstimate(flops=flops, bytes_accessed=moved, transcendentals=0),
    )(*args)


def prepare_body(features, centres, coefficients, rows, blocks, weights):
    rows[...] = features[...]
    blocks[...] = centres[...]
    weights[...] = coefficients[...].astype(BF16)


def prepare(features, centres, coefficients):
    outs = [jax.ShapeDtypeStruct(x.shape, BF16) for x in (features, centres, coefficients)]
    return whole_call(prepare_body, outs, [features, centres, coefficients])


def predict_body(nrow, ncen, nweight, first, *refs):
    rows, refs = refs[:nrow], refs[nrow:]
    blocks, refs = refs[:ncen], refs[ncen:]
    weights, refs = refs[:nweight], refs[nweight:]
    given, refs = ((), refs) if first else (refs[:nrow], refs[nrow:])
    kernel_ref, sums = refs[0], refs[1:]
    width = rows[0].shape[1]
    centres = jnp.concatenate([block[...] for block in blocks])
    coefs = jnp.concatenate([weight[...].astype(BF16) for weight in weights])
    dims = (((1,), (1,)), ((), ()))
    norms = jnp.sum(centres.astype(F32) ** 2, axis=1, keepdims=True)
    norms = jnp.transpose(jnp.broadcast_to(norms, (centres.shape[0], 128)))[:1]

    def tile(x, at):
        row_norms = jnp.sum(x.astype(F32) ** 2, axis=1, keepdims=True)
        products = lax.dot_general(x, centres, dims, preferred_element_type=F32)
        k = jnp.exp((2.0 * products - row_norms - norms) * (2.0 / width)).astype(BF16)
        kernel_ref[at, :] = k
        return jnp.dot(k, coefs, preferred_element_type=F32)

    sizes = [x.shape[0] for x in rows]
    if sum(sizes) <= 512:
        part = tile(jnp.concatenate([x[...] for x in rows]), slice(None))
        starts = [sum(sizes[:n]) for n in range(nrow)]
        for n, start in enumerate(starts):
            sums[n][...] = part[start : start + sizes[n]]
    else:
        base = 0
        for x, out in zip(rows, sums):
            chunk = min(512, x.shape[0])

            @pl.loop(0, x.shape[0] // chunk)
            def _(i, x=x, out=out, base=base, chunk=chunk):
                at = pl.ds(i * chunk, chunk)
                out[at, :] = tile(x[at, :], pl.ds(base + i * chunk, chunk))

            base += x.shape[0]
    for out, before in zip(sums, given):
        out[...] += before[...]


def predict(rows, blocks, given=(), flops=None):
    blocks, weights = blocks
    total = sum(x.shape[0] for x in rows)
    depth = sum(b.shape[0] for b in blocks)
    width = rows[0].shape[1]
    outs = weights[0].shape[1]
    shapes = [jax.ShapeDtypeStruct((total, depth), BF16)]
    shapes += [jax.ShapeDtypeStruct((x.shape[0], outs), F32) for x in rows]
    body = functools.partial(predict_body, len(rows), len(blocks), len(weights), not given)
    flops = flops or 2 * total * depth * (width + outs)
    kernel, *sums = whole_call(body, shapes, [*rows, *blocks, *weights, *given], flops=flops)
    return kernel, sums


def gradient_body(layout, npiece, first, *refs):
    kernels, refs = refs[: len(layout)], refs[len(layout) :]
    pieces, refs = refs[:npiece], refs[npiece:]
    if first:
        *outs, residual = refs
        base = 0
        for piece in [pieces[0], *pieces[:0:-1]]:
            residual[base : base + piece.shape[0], :] = piece[...]
            base += piece.shape[0]
    else:
        outs, residual = refs, pieces[0]
    started = set()
    for kernel, (first_row, first_block, blocks) in zip(kernels, layout):
        rows, order = kernel.shape[0], outs[0].shape[0]
        chunk = min(512, rows)
        for n, out in enumerate(blocks, first_block):

            def term(i, kernel=kernel, n=n, first_row=first_row, chunk=chunk):
                return lax.dot_general(
                    kernel[pl.ds(i * chunk, chunk), n * order : (n + 1) * order],
                    residual[pl.ds(first_row + i * chunk, chunk), :],
                    (((0,), (0,)), ((), ())),
                    preferred_element_type=F32,
                )

            if out in started:
                outs[out][...] += term(0)
            else:
                outs[out][...] = term(0)
                started.add(out)
            if rows > chunk:

                @pl.loop(1, rows // chunk)
                def _(i, out=out, term=term):
                    outs[out][...] += term(i)


def gradients(kernels, layout, pieces, count):
    total = sum(p.shape[0] for p in pieces)
    columns = pieces[0].shape[1]
    out = jax.ShapeDtypeStruct((count, columns), F32)
    joined = [jax.ShapeDtypeStruct((total, columns), BF16)] if len(pieces) > 1 else []
    body = functools.partial(gradient_body, layout, len(pieces), len(pieces) > 1)
    return whole_call(body, [out, out] + joined, [*kernels, pieces[0], *pieces[:0:-1]], flops=4 * total * count * columns)


def update_body(batch, npart, *refs):
    parts, refs = refs[:npart], refs[npart:]
    inverse, momentum, coefficients, residual, new_momentum, new_coefficients, out = refs
    out[...] = residual[...]
    gradient = parts[0][...]
    for part in parts[1:]:
        gradient += part[...]
    nblocks, order = inverse.shape[0], inverse.shape[1]
    for b in range(nblocks):
        at = slice(b * order, (b + 1) * order)
        conditioned = jnp.dot(
            inverse[b], gradient[at], precision=lax.Precision.HIGHEST, preferred_element_type=F32
        )
        moved = 0.9 * momentum[at, :] + conditioned / batch
        new_momentum[at, :] = moved
        new_coefficients[at, :] = coefficients[at, :] - 0.5 * moved


def shards(size, features, centres, targets, coefficients, momentum, block_inverse):
    batch = features.shape[0] * size
    count = centres.shape[0]
    core, far = 1, 2
    digits = digits_of([1 << b for b in range(1, size.bit_length() - 1) if 1 << b != far])
    send = functools.partial(swap, size=size)

    own_rows, *own = prepare(features, centres, coefficients)
    rows = relay_pieces(features, digits, size)
    if len(digits) == 1:
        rows[0] = own_rows
    far_parts = [send(part, far) for part in jnp.split(centres, 2)]
    far_coef = send(coefficients, far)
    near = [send(centres, core)], [send(coefficients, core)]
    own = own[:1], own[1:]
    kernel_a, sums_a = predict(rows, own, flops=4 * 10**9)
    kernel_b, sums_b = predict(rows, near, sums_a)
    far_parts, far_coef, rows[-2] = lax.optimization_barrier((far_parts, far_coef, rows[-2]))
    distant = far_parts + [send(x, core) for x in far_parts], [far_coef, send(far_coef, core)]
    kernel_c, sums = predict(rows, distant, sums_b)
    far_kernels, far_layout = [kernel_c], ((0, 0, (0, 1)),)
    near_kernels, near_layout = [kernel_a, kernel_b], ((0, 0, (0,)), (0, 0, (1,)))

    scale = 2.0 ** math.floor(math.log2(65504 / (5.05 * 4 * count)))
    for digit in reversed(digits):
        masks = masks_of(digit)
        if len(sums) == 1:
            sums = jnp.split(sums[0], len(masks))
        kind, factor = (jnp.float16, scale) if digit is digits[-1] else (F32, 1.0)
        sent = [(factor * part).astype(kind) for part in sums[1:]]
        got = [send(part, m).astype(F32) for m, part in zip(masks[1:], sent)]
        sums = [sums[0] + functools.reduce(jnp.add, got) / factor]
    residual = sums[0] - targets.astype(F32)
    half = residual.astype(BF16)
    held = jax.ShapeDtypeStruct(targets.shape, F32)
    residuals = gather_pieces(half, digits, size)

    far_keep, far_give, joined = gradients(far_kernels, far_layout, residuals, count)
    arrived = send(far_keep + send(far_give, core), far)
    keep, give = gradients(near_kernels, near_layout, [joined], count)
    parts = [keep, send(give, core), arrived]
    out = jax.ShapeDtypeStruct(momentum.shape, F32)
    new_momentum, new_coefficients, residual = whole_call(
        functools.partial(update_body, batch, len(parts)),
        [out, out, held],
        [*parts, block_inverse, momentum, coefficients, residual],
    )
    return residual, new_momentum, new_coefficients


def solution(mesh):
    one = P(("groups", "wide"), None)
    in_specs = (one, one, one, one, one, P(("groups", "wide"), None, None))
    return jax.shard_map(
        functools.partial(shards, mesh.shape["wide"]),
        mesh=mesh,
        in_specs=in_specs,
        out_specs=(one, one, one),
        check_vma=False,
    )
```

```python
import functools
import math

import jax
import jax.numpy as jnp
from jax import lax
from jax.experimental import pallas as pl
from jax.experimental.pallas import tpu as pltpu
from jax.sharding import PartitionSpec as P


F32, BF16 = jnp.float32, jnp.bfloat16
MIB = 1 << 20


def swap(x, mask, size):
    return lax.ppermute(x, "wide", [(i, i ^ mask) for i in range(size)])


def masks_of(bits):
    masks = [0]
    for bit in bits:
        masks += [m ^ bit for m in masks]
    return masks


def digits_of(bits):
    return [bits[i : i + 2] for i in range(0, len(bits), 2)]


def gather_pieces(x, digits, size):
    pieces = [x]
    for digit in digits:
        whole = pieces[0] if len(pieces) == 1 else jnp.concatenate(pieces)
        pieces = [whole] + [swap(whole, m, size) for m in masks_of(digit)[1:]]
    return pieces


def relay_pieces(x, digits, size):
    pieces = [x]
    for digit in digits:
        pieces = [pieces[0] if len(pieces) == 1 else jnp.concatenate(pieces)]
        if len(digit) == 2:
            far = swap(pieces[0], digit[1], size)
            pieces += [swap(pieces[0], digit[0], size), far, swap(far, digit[0], size)]
        else:
            pieces += [swap(pieces[0], digit[0], size)]
    return pieces


def nbytes(*arrays):
    return sum(a.size * a.dtype.itemsize for a in arrays)


def whole_call(body, outs, args, scratch=(), flops=0):
    moved = nbytes(*args, *outs)
    return pl.pallas_call(
        body,
        out_shape=outs,
        in_specs=[pl.BlockSpec(memory_space=pltpu.VMEM)] * len(args),
        out_specs=[pl.BlockSpec(memory_space=pltpu.VMEM)] * len(outs),
        scratch_shapes=scratch,
        compiler_params=pltpu.CompilerParams(vmem_limit_bytes=moved + 12 * MIB),
        cost_estimate=pl.CostEstimate(flops=flops, bytes_accessed=moved, transcendentals=0),
    )(*args)


def prepare_body(features, centres, coefficients, rows, blocks, weights):
    rows[...] = features[...]
    blocks[...] = centres[...]
    weights[...] = coefficients[...].astype(BF16)


def prepare(features, centres, coefficients):
    outs = [jax.ShapeDtypeStruct(x.shape, BF16) for x in (features, centres, coefficients)]
    return whole_call(prepare_body, outs, [features, centres, coefficients])


def predict_body(nrow, ncen, nweight, first, *refs):
    rows, refs = refs[:nrow], refs[nrow:]
    blocks, refs = refs[:ncen], refs[ncen:]
    weights, refs = refs[:nweight], refs[nweight:]
    given, refs = ((), refs) if first else (refs[:nrow], refs[nrow:])
    kernel_ref, sums = refs[0], refs[1:]
    width = rows[0].shape[1]
    centres = jnp.concatenate([block[...] for block in blocks])
    coefs = jnp.concatenate([weight[...].astype(BF16) for weight in weights])
    dims = (((1,), (1,)), ((), ()))
    norms = jnp.sum(centres.astype(F32) ** 2, axis=1, keepdims=True)
    norms = jnp.transpose(jnp.broadcast_to(norms, (centres.shape[0], 128)))[:1]

    def tile(x, at):
        row_norms = jnp.sum(x.astype(F32) ** 2, axis=1, keepdims=True)
        products = lax.dot_general(x, centres, dims, preferred_element_type=F32)
        k = jnp.exp((2.0 * products - row_norms - norms) * (2.0 / width)).astype(BF16)
        kernel_ref[at, :] = k
        return jnp.dot(k, coefs, preferred_element_type=F32)

    sizes = [x.shape[0] for x in rows]
    if sum(sizes) <= 512:
        part = tile(jnp.concatenate([x[...] for x in rows]), slice(None))
        starts = [sum(sizes[:n]) for n in range(nrow)]
        for n, start in enumerate(starts):
            sums[n][...] = part[start : start + sizes[n]]
    else:
        base = 0
        for x, out in zip(rows, sums):
            chunk = min(512, x.shape[0])

            @pl.loop(0, x.shape[0] // chunk)
            def _(i, x=x, out=out, base=base, chunk=chunk):
                at = pl.ds(i * chunk, chunk)
                out[at, :] = tile(x[at, :], pl.ds(base + i * chunk, chunk))

            base += x.shape[0]
    for out, before in zip(sums, given):
        out[...] += before[...]


def predict(rows, blocks, given=(), flops=None):
    blocks, weights = blocks
    total = sum(x.shape[0] for x in rows)
    depth = sum(b.shape[0] for b in blocks)
    width = rows[0].shape[1]
    outs = weights[0].shape[1]
    shapes = [jax.ShapeDtypeStruct((total, depth), BF16)]
    shapes += [jax.ShapeDtypeStruct((x.shape[0], outs), F32) for x in rows]
    body = functools.partial(predict_body, len(rows), len(blocks), len(weights), not given)
    flops = flops or 2 * total * depth * (width + outs)
    kernel, *sums = whole_call(body, shapes, [*rows, *blocks, *weights, *given], flops=flops)
    return kernel, sums


def gradient_body(layout, npiece, first, *refs):
    kernels, refs = refs[: len(layout)], refs[len(layout) :]
    pieces, refs = refs[:npiece], refs[npiece:]
    if first:
        *outs, residual = refs
        base = 0
        for piece in [pieces[0], *pieces[:0:-1]]:
            residual[base : base + piece.shape[0], :] = piece[...]
            base += piece.shape[0]
    else:
        outs, residual = refs, pieces[0]
    started = set()
    for kernel, (first_row, first_block, blocks) in zip(kernels, layout):
        rows, order = kernel.shape[0], outs[0].shape[0]
        chunk = min(512, rows)
        for n, out in enumerate(blocks, first_block):

            def term(i, kernel=kernel, n=n, first_row=first_row, chunk=chunk):
                return lax.dot_general(
                    kernel[pl.ds(i * chunk, chunk), n * order : (n + 1) * order],
                    residual[pl.ds(first_row + i * chunk, chunk), :],
                    (((0,), (0,)), ((), ())),
                    preferred_element_type=F32,
                )

            if out in started:
                outs[out][...] += term(0)
            else:
                outs[out][...] = term(0)
                started.add(out)
            if rows > chunk:

                @pl.loop(1, rows // chunk)
                def _(i, out=out, term=term):
                    outs[out][...] += term(i)


def gradients(kernels, layout, pieces, count):
    total = sum(p.shape[0] for p in pieces)
    columns = pieces[0].shape[1]
    out = jax.ShapeDtypeStruct((count, columns), F32)
    joined = [jax.ShapeDtypeStruct((total, columns), BF16)] if len(pieces) > 1 else []
    body = functools.partial(gradient_body, layout, len(pieces), len(pieces) > 1)
    return whole_call(body, [out, out] + joined, [*kernels, pieces[0], *pieces[:0:-1]], flops=4 * total * count * columns)


def update_body(batch, npart, *refs):
    parts, refs = refs[:npart], refs[npart:]
    inverse, momentum, coefficients, residual, new_momentum, new_coefficients, out = refs
    out[...] = residual[...]
    gradient = parts[0][...]
    for part in parts[1:]:
        gradient += part[...]
    nblocks, order = inverse.shape[0], inverse.shape[1]
    for b in range(nblocks):
        at = slice(b * order, (b + 1) * order)
        conditioned = jnp.dot(
            inverse[b], gradient[at], precision=lax.Precision.HIGHEST, preferred_element_type=F32
        )
        moved = 0.9 * momentum[at, :] + conditioned / batch
        new_momentum[at, :] = moved
        new_coefficients[at, :] = coefficients[at, :] - 0.5 * moved


def shards(size, features, centres, targets, coefficients, momentum, block_inverse):
    batch = features.shape[0] * size
    count = centres.shape[0]
    core, far = 1, 2
    digits = digits_of([1 << b for b in range(1, size.bit_length() - 1) if 1 << b != far])
    send = functools.partial(swap, size=size)

    own_rows, *own = prepare(features, centres, coefficients)
    rows = relay_pieces(features, digits, size)
    if len(digits) == 1:
        rows[0] = own_rows
    far_parts = [send(part, far) for part in jnp.split(centres, 2)]
    far_coef = send(coefficients, far)
    near = [send(centres, core)], [send(coefficients, core)]
    own = own[:1], own[1:]
    kernel_a, sums_a = predict(rows, own, flops=4 * 10**9)
    kernel_b, sums_b = predict(rows, near, sums_a)
    far_parts, far_coef, rows[-2] = lax.optimization_barrier((far_parts, far_coef, rows[-2]))
    distant = far_parts + [send(x, core) for x in far_parts], [far_coef, send(far_coef, core)]
    kernel_c, sums = predict(rows, distant, sums_b)
    far_kernels, far_layout = [kernel_c], ((0, 0, (0, 1)),)
    near_kernels, near_layout = [kernel_a, kernel_b], ((0, 0, (0,)), (0, 0, (1,)))

    scale = 2.0 ** math.floor(math.log2(65504 / (5.05 * 4 * count)))
    for digit in reversed(digits):
        masks = masks_of(digit)
        if len(sums) == 1:
            sums = jnp.split(sums[0], len(masks))
        kind, factor = (jnp.float16, scale) if digit is digits[-1] else (F32, 1.0)
        sent = [(factor * part).astype(kind) for part in sums[1:]]
        got = [send(part, m).astype(F32) for m, part in zip(masks[1:], sent)]
        sums = [sums[0] + functools.reduce(jnp.add, got) / factor]
    residual = sums[0] - targets.astype(F32)
    half = residual.astype(BF16)
    held = jax.ShapeDtypeStruct(targets.shape, F32)
    residuals = gather_pieces(half, digits, size)

    bound = 2 * sum(p.shape[0] for p in residuals) * (5.05 * size * count + 24)
    scale = 2.0 ** math.floor(math.log2(65504 / bound))
    kind, factor = (jnp.float16, scale) if scale >= 2.0**-10 else (F32, 1.0)
    far_keep, far_give, joined = gradients(far_kernels, far_layout, residuals, count)
    arrived = send((factor * (far_keep + send(far_give, core))).astype(kind), far).astype(F32) / factor
    keep, give = gradients(near_kernels, near_layout, [joined], count)
    parts = [keep, send(give, core), arrived]
    out = jax.ShapeDtypeStruct(momentum.shape, F32)
    new_momentum, new_coefficients, residual = whole_call(
        functools.partial(update_body, batch, len(parts)),
        [out, out, held],
        [*parts, block_inverse, momentum, coefficients, residual],
    )
    return residual, new_momentum, new_coefficients


def solution(mesh):
    one = P(("groups", "wide"), None)
    in_specs = (one, one, one, one, one, P(("groups", "wide"), None, None))
    return jax.shard_map(
        functools.partial(shards, mesh.shape["wide"]),
        mesh=mesh,
        in_specs=in_specs,
        out_specs=(one, one, one),
        check_vma=False,
    )
```

```python
import functools
import math

import jax
import jax.numpy as jnp
from jax import lax
from jax.experimental import pallas as pl
from jax.experimental.pallas import tpu as pltpu
from jax.sharding import PartitionSpec as P


F32, BF16 = jnp.float32, jnp.bfloat16
MIB = 1 << 20


def swap(x, mask, size):
    return lax.ppermute(x, "wide", [(i, i ^ mask) for i in range(size)])


def masks_of(bits):
    masks = [0]
    for bit in bits:
        masks += [m ^ bit for m in masks]
    return masks


def digits_of(bits):
    return [bits[i : i + 2] for i in range(0, len(bits), 2)]


def gather_pieces(x, digits, size):
    pieces = [x]
    for digit in digits:
        whole = pieces[0] if len(pieces) == 1 else jnp.concatenate(pieces)
        pieces = [whole] + [swap(whole, m, size) for m in masks_of(digit)[1:]]
    return pieces


def relay_pieces(x, digits, size):
    pieces = [x]
    for digit in digits:
        pieces = [pieces[0] if len(pieces) == 1 else jnp.concatenate(pieces)]
        if len(digit) == 2:
            far = swap(pieces[0], digit[1], size)
            pieces += [swap(pieces[0], digit[0], size), far, swap(far, digit[0], size)]
        else:
            pieces += [swap(pieces[0], digit[0], size)]
    return pieces


def nbytes(*arrays):
    return sum(a.size * a.dtype.itemsize for a in arrays)


def whole_call(body, outs, args, scratch=(), flops=0):
    moved = nbytes(*args, *outs)
    return pl.pallas_call(
        body,
        out_shape=outs,
        in_specs=[pl.BlockSpec(memory_space=pltpu.VMEM)] * len(args),
        out_specs=[pl.BlockSpec(memory_space=pltpu.VMEM)] * len(outs),
        scratch_shapes=scratch,
        compiler_params=pltpu.CompilerParams(vmem_limit_bytes=moved + 12 * MIB),
        cost_estimate=pl.CostEstimate(flops=flops, bytes_accessed=moved, transcendentals=0),
    )(*args)


def prepare_body(features, centres, coefficients, rows, blocks, weights):
    rows[...] = features[...]
    blocks[...] = centres[...]
    weights[...] = coefficients[...].astype(BF16)


def prepare(features, centres, coefficients):
    outs = [jax.ShapeDtypeStruct(x.shape, BF16) for x in (features, centres, coefficients)]
    return whole_call(prepare_body, outs, [features, centres, coefficients])


def predict_body(nrow, ncen, nweight, first, *refs):
    rows, refs = refs[:nrow], refs[nrow:]
    blocks, refs = refs[:ncen], refs[ncen:]
    weights, refs = refs[:nweight], refs[nweight:]
    given, refs = ((), refs) if first else (refs[:nrow], refs[nrow:])
    kernel_ref, sums = refs[0], refs[1:]
    width = rows[0].shape[1]
    centres = jnp.concatenate([block[...] for block in blocks])
    coefs = jnp.concatenate([weight[...].astype(BF16) for weight in weights])
    dims = (((1,), (1,)), ((), ()))
    norms = jnp.sum(centres.astype(F32) ** 2, axis=1, keepdims=True)
    norms = jnp.transpose(jnp.broadcast_to(norms, (centres.shape[0], 128)))[:1]

    def tile(x, at):
        row_norms = jnp.sum(x.astype(F32) ** 2, axis=1, keepdims=True)
        products = lax.dot_general(x, centres, dims, preferred_element_type=F32)
        k = jnp.exp((2.0 * products - row_norms - norms) * (2.0 / width)).astype(BF16)
        kernel_ref[at, :] = k
        return jnp.dot(k, coefs, preferred_element_type=F32)

    sizes = [x.shape[0] for x in rows]
    if sum(sizes) <= 512:
        part = tile(jnp.concatenate([x[...] for x in rows]), slice(None))
        starts = [sum(sizes[:n]) for n in range(nrow)]
        for n, start in enumerate(starts):
            sums[n][...] = part[start : start + sizes[n]]
    else:
        base = 0
        for x, out in zip(rows, sums):
            chunk = min(512, x.shape[0])

            @pl.loop(0, x.shape[0] // chunk)
            def _(i, x=x, out=out, base=base, chunk=chunk):
                at = pl.ds(i * chunk, chunk)
                out[at, :] = tile(x[at, :], pl.ds(base + i * chunk, chunk))

            base += x.shape[0]
    for out, before in zip(sums, given):
        out[...] += before[...]


def predict(rows, blocks, given=(), flops=None):
    blocks, weights = blocks
    total = sum(x.shape[0] for x in rows)
    depth = sum(b.shape[0] for b in blocks)
    width = rows[0].shape[1]
    outs = weights[0].shape[1]
    shapes = [jax.ShapeDtypeStruct((total, depth), BF16)]
    shapes += [jax.ShapeDtypeStruct((x.shape[0], outs), F32) for x in rows]
    body = functools.partial(predict_body, len(rows), len(blocks), len(weights), not given)
    flops = flops or 2 * total * depth * (width + outs)
    kernel, *sums = whole_call(body, shapes, [*rows, *blocks, *weights, *given], flops=flops)
    return kernel, sums


def gradient_body(layout, npiece, first, *refs):
    kernels, refs = refs[: len(layout)], refs[len(layout) :]
    pieces, refs = refs[:npiece], refs[npiece:]
    if first:
        *outs, residual = refs
        base = 0
        for piece in [pieces[0], *pieces[:0:-1]]:
            residual[base : base + piece.shape[0], :] = piece[...]
            base += piece.shape[0]
    else:
        outs, residual = refs, pieces[0]
    started = set()
    for kernel, (first_row, first_block, blocks) in zip(kernels, layout):
        rows, order = kernel.shape[0], outs[0].shape[0]
        chunk = min(512, rows)
        for n, out in enumerate(blocks, first_block):

            def term(i, kernel=kernel, n=n, first_row=first_row, chunk=chunk):
                return lax.dot_general(
                    kernel[pl.ds(i * chunk, chunk), n * order : (n + 1) * order],
                    residual[pl.ds(first_row + i * chunk, chunk), :],
                    (((0,), (0,)), ((), ())),
                    preferred_element_type=F32,
                )

            if out in started:
                outs[out][...] += term(0)
            else:
                outs[out][...] = term(0)
                started.add(out)
            if rows > chunk:

                @pl.loop(1, rows // chunk)
                def _(i, out=out, term=term):
                    outs[out][...] += term(i)


def gradients(kernels, layout, pieces, count):
    total = sum(p.shape[0] for p in pieces)
    columns = pieces[0].shape[1]
    out = jax.ShapeDtypeStruct((count, columns), F32)
    joined = [jax.ShapeDtypeStruct((total, columns), BF16)] if len(pieces) > 1 else []
    body = functools.partial(gradient_body, layout, len(pieces), len(pieces) > 1)
    return whole_call(body, [out, out] + joined, [*kernels, pieces[0], *pieces[:0:-1]], flops=4 * total * count * columns)


def update_body(batch, npart, *refs):
    parts, refs = refs[:npart], refs[npart:]
    inverse, momentum, coefficients, residual, new_momentum, new_coefficients, out = refs
    out[...] = residual[...]
    gradient = parts[0][...]
    for part in parts[1:]:
        gradient += part[...]
    nblocks, order = inverse.shape[0], inverse.shape[1]
    for b in range(nblocks):
        at = slice(b * order, (b + 1) * order)
        conditioned = jnp.dot(
            inverse[b], gradient[at], precision=lax.Precision.HIGHEST, preferred_element_type=F32
        )
        moved = 0.9 * momentum[at, :] + conditioned / batch
        new_momentum[at, :] = moved
        new_coefficients[at, :] = coefficients[at, :] - 0.5 * moved


def shards(size, features, centres, targets, coefficients, momentum, block_inverse):
    batch = features.shape[0] * size
    count = centres.shape[0]
    core, far = 1, 2
    digits = digits_of([1 << b for b in range(1, size.bit_length() - 1) if 1 << b != far])
    send = functools.partial(swap, size=size)

    own_rows, *own = prepare(features, centres, coefficients)
    rows = relay_pieces(features, digits, size)
    if len(digits) == 1:
        rows[0] = own_rows
    far_parts = [send(part, far) for part in jnp.split(centres, 2)]
    far_coef = send(coefficients, far)
    near = [send(centres, core)], [send(coefficients, core)]
    own = own[:1], own[1:]
    kernel_a, sums_a = predict(rows, own, flops=8 * 10**9)
    kernel_b, sums_b = predict(rows, near, sums_a)
    far_parts, rows[-2] = lax.optimization_barrier((far_parts, rows[-2]))
    distant = far_parts + [send(x, core) for x in far_parts], [far_coef, send(far_coef, core)]
    kernel_c, sums = predict(rows, distant, sums_b)
    far_kernels, far_layout = [kernel_c], ((0, 0, (0, 1)),)
    near_kernels, near_layout = [kernel_a, kernel_b], ((0, 0, (0,)), (0, 0, (1,)))

    scale = 2.0 ** math.floor(math.log2(65504 / (5.05 * 4 * count)))
    for digit in reversed(digits):
        masks = masks_of(digit)
        if len(sums) == 1:
            sums = jnp.split(sums[0], len(masks))
        kind, factor = (jnp.float16, scale) if digit is digits[-1] else (F32, 1.0)
        sent = [(factor * part).astype(kind) for part in sums[1:]]
        got = [send(part, m).astype(F32) for m, part in zip(masks[1:], sent)]
        sums = [sums[0] + functools.reduce(jnp.add, got) / factor]
    residual = sums[0] - targets.astype(F32)
    half = residual.astype(BF16)
    held = jax.ShapeDtypeStruct(targets.shape, F32)
    residuals = gather_pieces(half, digits, size)

    bound = 2 * sum(p.shape[0] for p in residuals) * (5.05 * size * count + 24)
    scale = 2.0 ** math.floor(math.log2(65504 / bound))
    kind, factor = (jnp.float16, scale) if scale >= 2.0**-10 else (F32, 1.0)
    far_keep, far_give, joined = gradients(far_kernels, far_layout, residuals, count)
    arrived = send((factor * (far_keep + send(far_give, core))).astype(kind), far).astype(F32) / factor
    keep, give = gradients(near_kernels, near_layout, [joined], count)
    parts = [keep, send(give, core), arrived]
    out = jax.ShapeDtypeStruct(momentum.shape, F32)
    new_momentum, new_coefficients, residual = whole_call(
        functools.partial(update_body, batch, len(parts)),
        [out, out, held],
        [*parts, block_inverse, momentum, coefficients, residual],
    )
    return residual, new_momentum, new_coefficients


def solution(mesh):
    one = P(("groups", "wide"), None)
    in_specs = (one, one, one, one, one, P(("groups", "wide"), None, None))
    return jax.shard_map(
        functools.partial(shards, mesh.shape["wide"]),
        mesh=mesh,
        in_specs=in_specs,
        out_specs=(one, one, one),
        check_vma=False,
    )
```

```python
import functools
import math

import jax
import jax.numpy as jnp
from jax import lax
from jax.experimental import pallas as pl
from jax.experimental.pallas import tpu as pltpu
from jax.sharding import PartitionSpec as P


F32, BF16 = jnp.float32, jnp.bfloat16
MIB = 1 << 20


def swap(x, mask, size):
    return lax.ppermute(x, "wide", [(i, i ^ mask) for i in range(size)])


def masks_of(bits):
    masks = [0]
    for bit in bits:
        masks += [m ^ bit for m in masks]
    return masks


def digits_of(bits):
    return [bits[i : i + 2] for i in range(0, len(bits), 2)]


def gather_pieces(x, digits, size):
    pieces = [x]
    for digit in digits:
        whole = pieces[0] if len(pieces) == 1 else jnp.concatenate(pieces)
        pieces = [whole] + [swap(whole, m, size) for m in masks_of(digit)[1:]]
    return pieces


def relay_pieces(x, digits, size):
    pieces = [x]
    for digit in digits:
        pieces = [pieces[0] if len(pieces) == 1 else jnp.concatenate(pieces)]
        if len(digit) == 2:
            far = swap(pieces[0], digit[1], size)
            pieces += [swap(pieces[0], digit[0], size), far, swap(far, digit[0], size)]
        else:
            pieces += [swap(pieces[0], digit[0], size)]
    return pieces


def nbytes(*arrays):
    return sum(a.size * a.dtype.itemsize for a in arrays)


def whole_call(body, outs, args, scratch=(), flops=0):
    moved = nbytes(*args, *outs)
    return pl.pallas_call(
        body,
        out_shape=outs,
        in_specs=[pl.BlockSpec(memory_space=pltpu.VMEM)] * len(args),
        out_specs=[pl.BlockSpec(memory_space=pltpu.VMEM)] * len(outs),
        scratch_shapes=scratch,
        compiler_params=pltpu.CompilerParams(vmem_limit_bytes=moved + 12 * MIB),
        cost_estimate=pl.CostEstimate(flops=flops, bytes_accessed=moved, transcendentals=0),
    )(*args)


def prepare_body(features, centres, coefficients, rows, blocks, weights):
    rows[...] = features[...]
    blocks[...] = centres[...]
    weights[...] = coefficients[...].astype(BF16)


def prepare(features, centres, coefficients):
    outs = [jax.ShapeDtypeStruct(x.shape, BF16) for x in (features, centres, coefficients)]
    return whole_call(prepare_body, outs, [features, centres, coefficients])


def predict_body(nrow, ncen, nweight, first, *refs):
    rows, refs = refs[:nrow], refs[nrow:]
    blocks, refs = refs[:ncen], refs[ncen:]
    weights, refs = refs[:nweight], refs[nweight:]
    given, refs = ((), refs) if first else (refs[:nrow], refs[nrow:])
    kernel_ref, sums = refs[0], refs[1:]
    width = rows[0].shape[1]
    centres = jnp.concatenate([block[...] for block in blocks])
    coefs = jnp.concatenate([weight[...].astype(BF16) for weight in weights])
    dims = (((1,), (1,)), ((), ()))
    norms = jnp.sum(centres.astype(F32) ** 2, axis=1, keepdims=True)
    norms = jnp.transpose(jnp.broadcast_to(norms, (centres.shape[0], 128)))[:1]

    def tile(x, at):
        row_norms = jnp.sum(x.astype(F32) ** 2, axis=1, keepdims=True)
        products = lax.dot_general(x, centres, dims, preferred_element_type=F32)
        k = jnp.exp((2.0 * products - row_norms - norms) * (2.0 / width)).astype(BF16)
        kernel_ref[at, :] = k
        return jnp.dot(k, coefs, preferred_element_type=F32)

    sizes = [x.shape[0] for x in rows]
    if sum(sizes) <= 512:
        part = tile(jnp.concatenate([x[...] for x in rows]), slice(None))
        starts = [sum(sizes[:n]) for n in range(nrow)]
        for n, start in enumerate(starts):
            sums[n][...] = part[start : start + sizes[n]]
    else:
        base = 0
        for x, out in zip(rows, sums):
            chunk = min(512, x.shape[0])

            @pl.loop(0, x.shape[0] // chunk)
            def _(i, x=x, out=out, base=base, chunk=chunk):
                at = pl.ds(i * chunk, chunk)
                out[at, :] = tile(x[at, :], pl.ds(base + i * chunk, chunk))

            base += x.shape[0]
    for out, before in zip(sums, given):
        out[...] += before[...]


def predict(rows, blocks, given=(), flops=None):
    blocks, weights = blocks
    total = sum(x.shape[0] for x in rows)
    depth = sum(b.shape[0] for b in blocks)
    width = rows[0].shape[1]
    outs = weights[0].shape[1]
    shapes = [jax.ShapeDtypeStruct((total, depth), BF16)]
    shapes += [jax.ShapeDtypeStruct((x.shape[0], outs), F32) for x in rows]
    body = functools.partial(predict_body, len(rows), len(blocks), len(weights), not given)
    flops = flops or 2 * total * depth * (width + outs)
    kernel, *sums = whole_call(body, shapes, [*rows, *blocks, *weights, *given], flops=flops)
    return kernel, sums


def gradient_body(layout, npiece, first, *refs):
    kernels, refs = refs[: len(layout)], refs[len(layout) :]
    pieces, refs = refs[:npiece], refs[npiece:]
    if first:
        *outs, residual = refs
        base = 0
        for piece in [pieces[0], *pieces[:0:-1]]:
            residual[base : base + piece.shape[0], :] = piece[...]
            base += piece.shape[0]
    else:
        outs, residual = refs, pieces[0]
    started = set()
    for kernel, (first_row, first_block, blocks) in zip(kernels, layout):
        rows, order = kernel.shape[0], outs[0].shape[0]
        chunk = min(512, rows)
        for n, out in enumerate(blocks, first_block):

            def term(i, kernel=kernel, n=n, first_row=first_row, chunk=chunk):
                return lax.dot_general(
                    kernel[pl.ds(i * chunk, chunk), n * order : (n + 1) * order],
                    residual[pl.ds(first_row + i * chunk, chunk), :],
                    (((0,), (0,)), ((), ())),
                    preferred_element_type=F32,
                )

            if out in started:
                outs[out][...] += term(0)
            else:
                outs[out][...] = term(0)
                started.add(out)
            if rows > chunk:

                @pl.loop(1, rows // chunk)
                def _(i, out=out, term=term):
                    outs[out][...] += term(i)


def gradients(kernels, layout, pieces, count):
    total = sum(p.shape[0] for p in pieces)
    columns = pieces[0].shape[1]
    out = jax.ShapeDtypeStruct((count, columns), F32)
    joined = [jax.ShapeDtypeStruct((total, columns), BF16)] if len(pieces) > 1 else []
    body = functools.partial(gradient_body, layout, len(pieces), len(pieces) > 1)
    return whole_call(body, [out, out] + joined, [*kernels, pieces[0], *pieces[:0:-1]], flops=4 * total * count * columns)


def product(inverse, gradient, b):
    order = inverse.shape[1]
    at = slice(b * order, (b + 1) * order)
    return at, jnp.dot(inverse[b], gradient[at, :], precision=lax.Precision.HIGHEST, preferred_element_type=F32)


def begin_body(batch, keep, got, inverse, momentum, residual, begun, out):
    out[...] = residual[...]
    gradient = keep[...] + got[...]
    for b in range(inverse.shape[0]):
        at, conditioned = product(inverse, gradient, b)
        begun[at, :] = 0.9 * momentum[at, :] + conditioned / batch


def update_body(batch, arrived, inverse, begun, coefficients, new_momentum, new_coefficients):
    for b in range(inverse.shape[0]):
        at, conditioned = product(inverse, arrived[...], b)
        moved = begun[at, :] + conditioned / batch
        new_momentum[at, :] = moved
        new_coefficients[at, :] = coefficients[at, :] - 0.5 * moved


def shards(size, features, centres, targets, coefficients, momentum, block_inverse):
    batch = features.shape[0] * size
    count = centres.shape[0]
    core, far = 1, 2
    digits = digits_of([1 << b for b in range(1, size.bit_length() - 1) if 1 << b != far])
    send = functools.partial(swap, size=size)

    own_rows, *own = prepare(features, centres, coefficients)
    rows = relay_pieces(features, digits, size)
    if len(digits) == 1:
        rows[0] = own_rows
    far_parts = [send(part, far) for part in jnp.split(centres, 2)]
    far_coef = send(coefficients, far)
    near = [send(centres, core)], [send(coefficients, core)]
    own = own[:1], own[1:]
    kernel_a, sums_a = predict(rows, own, flops=8 * 10**9)
    kernel_b, sums_b = predict(rows, near, sums_a)
    far_parts, rows[-2] = lax.optimization_barrier((far_parts, rows[-2]))
    distant = far_parts + [send(x, core) for x in far_parts], [far_coef, send(far_coef, core)]
    kernel_c, sums = predict(rows, distant, sums_b)
    far_kernels, far_layout = [kernel_c], ((0, 0, (0, 1)),)
    near_kernels, near_layout = [kernel_a, kernel_b], ((0, 0, (0,)), (0, 0, (1,)))

    scale = 2.0 ** math.floor(math.log2(65504 / (5.05 * 4 * count)))
    for digit in reversed(digits):
        masks = masks_of(digit)
        if len(sums) == 1:
            sums = jnp.split(sums[0], len(masks))
        kind, factor = (jnp.float16, scale) if digit is digits[-1] else (F32, 1.0)
        sent = [(factor * part).astype(kind) for part in sums[1:]]
        got = [send(part, m).astype(F32) for m, part in zip(masks[1:], sent)]
        sums = [sums[0] + functools.reduce(jnp.add, got) / factor]
    residual = sums[0] - targets.astype(F32)
    half = residual.astype(BF16)
    held = jax.ShapeDtypeStruct(targets.shape, F32)
    residuals = gather_pieces(half, digits, size)

    bound = 2 * sum(p.shape[0] for p in residuals) * (5.05 * size * count + 24)
    scale = 2.0 ** math.floor(math.log2(65504 / bound))
    kind, factor = (jnp.float16, scale) if scale >= 2.0**-10 else (F32, 1.0)
    far_keep, far_give, joined = gradients(far_kernels, far_layout, residuals, count)
    arrived = send((factor * (far_keep + send(far_give, core))).astype(kind), far).astype(F32) / factor
    keep, give = gradients(near_kernels, near_layout, [joined], count)
    out = jax.ShapeDtypeStruct(momentum.shape, F32)
    begun, residual = whole_call(
        functools.partial(begin_body, batch),
        [out, held],
        [keep, send(give, core), block_inverse, momentum, residual],
    )
    new_momentum, new_coefficients = whole_call(
        functools.partial(update_body, batch), [out, out], [arrived, block_inverse, begun, coefficients]
    )
    return residual, new_momentum, new_coefficients


def solution(mesh):
    one = P(("groups", "wide"), None)
    in_specs = (one, one, one, one, one, P(("groups", "wide"), None, None))
    return jax.shard_map(
        functools.partial(shards, mesh.shape["wide"]),
        mesh=mesh,
        in_specs=in_specs,
        out_specs=(one, one, one),
        check_vma=False,
    )
```

```python
import functools
import math

import jax
import jax.numpy as jnp
from jax import lax
from jax.experimental import pallas as pl
from jax.experimental.pallas import tpu as pltpu
from jax.sharding import PartitionSpec as P


F32, BF16 = jnp.float32, jnp.bfloat16
MIB = 1 << 20


def swap(x, mask, size):
    return lax.ppermute(x, "wide", [(i, i ^ mask) for i in range(size)])


def masks_of(bits):
    masks = [0]
    for bit in bits:
        masks += [m ^ bit for m in masks]
    return masks


def digits_of(bits):
    return [bits[i : i + 2] for i in range(0, len(bits), 2)]


def gather_pieces(x, digits, size):
    pieces = [x]
    for digit in digits:
        whole = pieces[0] if len(pieces) == 1 else jnp.concatenate(pieces)
        pieces = [whole] + [swap(whole, m, size) for m in masks_of(digit)[1:]]
    return pieces


def relay_pieces(x, digits, size):
    pieces = [x]
    for digit in digits:
        pieces = [pieces[0] if len(pieces) == 1 else jnp.concatenate(pieces)]
        if len(digit) == 2:
            far = swap(pieces[0], digit[1], size)
            pieces += [swap(pieces[0], digit[0], size), far, swap(far, digit[0], size)]
        else:
            pieces += [swap(pieces[0], digit[0], size)]
    return pieces


def nbytes(*arrays):
    return sum(a.size * a.dtype.itemsize for a in arrays)


def whole_call(body, outs, args, scratch=(), flops=0):
    moved = nbytes(*args, *outs)
    return pl.pallas_call(
        body,
        out_shape=outs,
        in_specs=[pl.BlockSpec(memory_space=pltpu.VMEM)] * len(args),
        out_specs=[pl.BlockSpec(memory_space=pltpu.VMEM)] * len(outs),
        scratch_shapes=scratch,
        compiler_params=pltpu.CompilerParams(vmem_limit_bytes=moved + 12 * MIB),
        cost_estimate=pl.CostEstimate(flops=flops, bytes_accessed=moved, transcendentals=0),
    )(*args)


def prepare_body(features, centres, coefficients, rows, blocks, weights):
    rows[...] = features[...]
    blocks[...] = centres[...]
    weights[...] = coefficients[...].astype(BF16)


def prepare(features, centres, coefficients):
    outs = [jax.ShapeDtypeStruct(x.shape, BF16) for x in (features, centres, coefficients)]
    return whole_call(prepare_body, outs, [features, centres, coefficients])


def predict_body(nrow, ncen, nweight, first, *refs):
    rows, refs = refs[:nrow], refs[nrow:]
    blocks, refs = refs[:ncen], refs[ncen:]
    weights, refs = refs[:nweight], refs[nweight:]
    given, refs = ((), refs) if first else (refs[:nrow], refs[nrow:])
    kernel_ref, sums = refs[0], refs[1:]
    width = rows[0].shape[1]
    centres = jnp.concatenate([block[...] for block in blocks])
    coefs = jnp.concatenate([weight[...].astype(BF16) for weight in weights])
    dims = (((1,), (1,)), ((), ()))
    norms = jnp.sum(centres.astype(F32) ** 2, axis=1, keepdims=True)
    norms = jnp.transpose(jnp.broadcast_to(norms, (centres.shape[0], 128)))[:1]

    def tile(x, at):
        row_norms = jnp.sum(x.astype(F32) ** 2, axis=1, keepdims=True)
        products = lax.dot_general(x, centres, dims, preferred_element_type=F32)
        k = jnp.exp((2.0 * products - row_norms - norms) * (2.0 / width)).astype(BF16)
        kernel_ref[at, :] = k
        return jnp.dot(k, coefs, preferred_element_type=F32)

    sizes = [x.shape[0] for x in rows]
    if sum(sizes) <= 512:
        part = tile(jnp.concatenate([x[...] for x in rows]), slice(None))
        starts = [sum(sizes[:n]) for n in range(nrow)]
        for n, start in enumerate(starts):
            sums[n][...] = part[start : start + sizes[n]]
    else:
        base = 0
        for x, out in zip(rows, sums):
            chunk = min(512, x.shape[0])

            @pl.loop(0, x.shape[0] // chunk)
            def _(i, x=x, out=out, base=base, chunk=chunk):
                at = pl.ds(i * chunk, chunk)
                out[at, :] = tile(x[at, :], pl.ds(base + i * chunk, chunk))

            base += x.shape[0]
    for out, before in zip(sums, given):
        out[...] += before[...]


def predict(rows, blocks, given=(), flops=None):
    blocks, weights = blocks
    total = sum(x.shape[0] for x in rows)
    depth = sum(b.shape[0] for b in blocks)
    width = rows[0].shape[1]
    outs = weights[0].shape[1]
    shapes = [jax.ShapeDtypeStruct((total, depth), BF16)]
    shapes += [jax.ShapeDtypeStruct((x.shape[0], outs), F32) for x in rows]
    body = functools.partial(predict_body, len(rows), len(blocks), len(weights), not given)
    flops = flops or 2 * total * depth * (width + outs)
    kernel, *sums = whole_call(body, shapes, [*rows, *blocks, *weights, *given], flops=flops)
    return kernel, sums


def gradient_body(layout, npiece, first, *refs):
    kernels, refs = refs[: len(layout)], refs[len(layout) :]
    pieces, refs = refs[:npiece], refs[npiece:]
    if first:
        *outs, residual = refs
        base = 0
        for piece in [pieces[0], *pieces[:0:-1]]:
            residual[base : base + piece.shape[0], :] = piece[...]
            base += piece.shape[0]
    else:
        outs, residual = refs, pieces[0]
    started = set()
    for kernel, (first_row, first_block, blocks) in zip(kernels, layout):
        rows, order = kernel.shape[0], outs[0].shape[0]
        chunk = min(512, rows)
        for n, out in enumerate(blocks, first_block):

            def term(i, kernel=kernel, n=n, first_row=first_row, chunk=chunk):
                return lax.dot_general(
                    kernel[pl.ds(i * chunk, chunk), n * order : (n + 1) * order],
                    residual[pl.ds(first_row + i * chunk, chunk), :],
                    (((0,), (0,)), ((), ())),
                    preferred_element_type=F32,
                )

            if out in started:
                outs[out][...] += term(0)
            else:
                outs[out][...] = term(0)
                started.add(out)
            if rows > chunk:

                @pl.loop(1, rows // chunk)
                def _(i, out=out, term=term):
                    outs[out][...] += term(i)


def gradients(kernels, layout, pieces, count):
    total = sum(p.shape[0] for p in pieces)
    columns = pieces[0].shape[1]
    out = jax.ShapeDtypeStruct((count, columns), F32)
    joined = [jax.ShapeDtypeStruct((total, columns), BF16)] if len(pieces) > 1 else []
    body = functools.partial(gradient_body, layout, len(pieces), len(pieces) > 1)
    return whole_call(body, [out, out] + joined, [*kernels, pieces[0], *pieces[:0:-1]], flops=4 * total * count * columns)


def update_body(batch, npart, *refs):
    parts, refs = refs[:npart], refs[npart:]
    inverse, momentum, coefficients, residual, new_momentum, new_coefficients, out = refs
    out[...] = residual[...]
    gradient = parts[0][...]
    for part in parts[1:]:
        gradient += part[...]
    nblocks, order = inverse.shape[0], inverse.shape[1]
    for b in range(nblocks):
        at = slice(b * order, (b + 1) * order)
        conditioned = jnp.dot(
            inverse[b], gradient[at], precision=lax.Precision.HIGHEST, preferred_element_type=F32
        )
        moved = 0.9 * momentum[at, :] + conditioned / batch
        new_momentum[at, :] = moved
        new_coefficients[at, :] = coefficients[at, :] - 0.5 * moved


def shards(size, features, centres, targets, coefficients, momentum, block_inverse):
    batch = features.shape[0] * size
    count = centres.shape[0]
    core, far = 1, 2
    digits = digits_of([1 << b for b in range(1, size.bit_length() - 1) if 1 << b != far])
    send = functools.partial(swap, size=size)

    own_rows, *own = prepare(features, centres, coefficients)
    rows = relay_pieces(features, digits, size)
    if len(digits) == 1:
        rows[0] = own_rows
    far_parts = [send(part, far) for part in jnp.split(centres, 2)]
    far_coef = send(coefficients, far)
    near = [send(centres, core)], [send(coefficients, core)]
    own = own[:1], own[1:]
    kernel_a, sums_a = predict(rows, own, flops=8 * 10**9)
    kernel_b, sums_b = predict(rows, near, sums_a)
    far_parts, rows[-2] = lax.optimization_barrier((far_parts, rows[-2]))
    distant = far_parts + [send(x, core) for x in far_parts], [far_coef, send(far_coef, core)]
    kernel_c, sums = predict(rows, distant, sums_b)
    far_kernels, far_layout = [kernel_c], ((0, 0, (0, 1)),)
    near_kernels, near_layout = [kernel_a, kernel_b], ((0, 0, (0,)), (0, 0, (1,)))

    scale = 2.0 ** math.floor(math.log2(65504 / (5.05 * 4 * count)))
    for digit in reversed(digits):
        masks = masks_of(digit)
        if len(sums) == 1:
            sums = jnp.split(sums[0], len(masks))
        kind, factor = (jnp.float16, scale) if digit is digits[-1] else (F32, 1.0)
        sent = [(factor * part).astype(kind) for part in sums[1:]]
        got = [send(part, m).astype(F32) for m, part in zip(masks[1:], sent)]
        sums = [sums[0] + functools.reduce(jnp.add, got) / factor]
    residual = sums[0] - targets.astype(F32)
    half = residual.astype(BF16)
    held = jax.ShapeDtypeStruct(targets.shape, F32)
    residuals = gather_pieces(half, digits, size)

    bound = 2 * sum(p.shape[0] for p in residuals) * (5.05 * size * count + 24)
    scale = 2.0 ** math.floor(math.log2(65504 / bound))
    kind, factor = (jnp.float16, scale) if scale >= 2.0**-10 else (F32, 1.0)
    far_keep, far_give, joined = gradients(far_kernels, far_layout, residuals, count)
    arrived = send((factor * (far_keep + send((factor * far_give).astype(kind), core).astype(F32) / factor)).astype(kind), far).astype(F32) / factor
    keep, give = gradients(near_kernels, near_layout, [joined], count)
    parts = [keep, send(give, core), arrived]
    out = jax.ShapeDtypeStruct(momentum.shape, F32)
    new_momentum, new_coefficients, residual = whole_call(
        functools.partial(update_body, batch, len(parts)),
        [out, out, held],
        [*parts, block_inverse, momentum, coefficients, residual],
    )
    return residual, new_momentum, new_coefficients


def solution(mesh):
    one = P(("groups", "wide"), None)
    in_specs = (one, one, one, one, one, P(("groups", "wide"), None, None))
    return jax.shard_map(
        functools.partial(shards, mesh.shape["wide"]),
        mesh=mesh,
        in_specs=in_specs,
        out_specs=(one, one, one),
        check_vma=False,
    )
```
